512 devices in a mesh: dp: 128 (over y, z, core), space: 4 (over x).
Axes of the slice: x: 4, y: 8, z: 8, core: 2. Of those that a mesh axis runs over, the one named last changes fastest.
Arguments:
- clips: bfloat16 [256, 4, 16, 32, 128], P('dp', None, 'space'), may hold values from -6 to 6
- lengths: int32 [256], P('dp'), may hold values from 1 to 2
- partner: int32 [1], replicated, may hold values from 1 to 127
- kernel: bfloat16 [3, 3, 3, 128, 128], replicated, may hold values from -0.109375 to 0.109375
- cot_stay: bfloat16 [128, 2, 16, 32, 128], P('dp', None, 'space'), may hold values from -6 to 6
- cot_guest: bfloat16 [128, 2, 16, 32, 128], P('dp', None, 'space'), may hold values from -6 to 6
Outputs:
- stay_out: bfloat16 [128, 2, 16, 32, 128], P('dp', None, 'space')
- guest_out: bfloat16 [128, 2, 16, 32, 128], P('dp', None, 'space')
- slab_grad: bfloat16 [256, 4, 16, 32, 128], P('dp', None, 'space')
- weight_grad: float32 [3, 3, 3, 128, 128], replicated
The draws below stay inside these ranges and needn't reach their ends.
Inputs may be any that keep to these rules, and one draw needn't show every extreme that they name: `partner`: one offset for the whole mesh.
All inputs are finite; a program needn't handle non-finite values.
Results may differ from the reference program's by a relative error of at most 0.0049.
Values may be sent and summed in bfloat16 or wider, within the bound.
No kernel may reach another device: no remote copies, remote signals or barrier semaphores. Data moves between devices by JAX's collectives and lax.ppermute only.
A program may use at most 64 MiB of HBM per device.

```python
import math
import jax
import jax.numpy as jnp
from jax import lax

C = 128
SF = 2
W = 32
NSLAB = 256
H = 16
N_DP = 128


def set_ends(array, key, low, high):
    spot = [jax.random.randint(jax.random.fold_in(key, axis), (), 0, length) for axis, length in enumerate(array.shape)]
    longest = array.shape.index(max(array.shape))
    beside = spot[:longest] + [(spot[longest] + 1) % array.shape[longest]] + spot[longest + 1:]
    return array.at[tuple(spot)].set(low).at[tuple(beside)].set(high)


def steps_of(key, shape, shards, least, top_value):
    loudness, own = 1.0, jax.random.fold_in(key, 6)
    for axis_at, blocks in shards:
        heights = jnp.exp(jax.random.uniform(jax.random.fold_in(own, axis_at), (blocks,), jnp.float32, least / len(shards), top_value / len(shards)))
        loudness = loudness * jnp.repeat(heights, shape[axis_at] // blocks).reshape([-1 if axis == axis_at else 1 for axis in range(len(shape))])
    return loudness


def noise(rng, shape, deviation, reach, pieces=(), held_as=jnp.bfloat16):
    entries = jax.random.normal(rng, shape, jnp.float32) * deviation
    if len(pieces) > 0:
        entries = steps_of(rng, shape, pieces, -0.22, 0.18) * entries
    return jnp.clip(entries, min=-reach, max=reach).astype(held_as)


def setup_inputs(seed: int = 0) -> dict:
    key_of = jax.random.split(jax.random.key(seed), 7)
    clips = noise(key_of[0], (NSLAB, SF + 2, H, W, C), 1.0, 6.0, ((0, 128), (2, 4)))
    lengths = set_ends(jax.random.randint(key_of[1], (NSLAB,), 1, SF + 1), jax.random.fold_in(key_of[1], 1), 1, SF).astype(jnp.int32)
    partner = jax.random.randint(key_of[2], (1,), 1, N_DP).astype(jnp.int32)
    kernel = noise(key_of[3], (3, 3, 3, C, C), (27 * C) ** -0.5, 0.109375)
    cot_stay = noise(key_of[4], (N_DP, SF, H, W, C), 1.0, 6.0, ((0, 128), (2, 4)))
    cot_guest = noise(key_of[5], (N_DP, SF, H, W, C), 1.0, 6.0, ((0, 128), (2, 4)))
    return {"clips": clips, "lengths": lengths, "partner": partner, "kernel": kernel, "cot_stay": cot_stay, "cot_guest": cot_guest}


def conv_full(inputs, weights):
    return lax.conv_general_dilated(inputs, weights, (1, 1, 1), ((0, 0), (1, 1), (1, 1)), dimension_numbers=('NDHWC', 'DHWIO', 'NDHWC'), precision=lax.Precision.HIGHEST)

def reference(clips, lengths, partner, kernel, cot_stay, cot_guest):
    index = jnp.arange(N_DP, dtype=jnp.int32)
    mates = jnp.bitwise_xor(index, partner[0].astype(jnp.int32))
    cots = jnp.stack([cot_stay, cot_guest[mates]], axis=1).reshape(NSLAB, SF, H, W, C)
    weights = kernel.astype(jnp.float32)
    groups = NSLAB // 4

    def one_group(items):
        inputs, grads_in, counts = items
        inputs = inputs.astype(jnp.float32)
        z_val, pull = jax.vjp(conv_full, inputs, weights)
        valid = (jnp.arange(SF, dtype=jnp.int32)[None, :] < counts[:, None]).astype(jnp.float32)
        valid = valid[:, :, None, None, None]
        sig = jax.nn.sigmoid(z_val)
        outputs = (valid * z_val * sig).astype(jnp.bfloat16)
        dz_val = (valid * grads_in.astype(jnp.float32) * sig * (1.0 + z_val * (1.0 - sig))).astype(jnp.bfloat16)
        dx_val, dw_val = pull(dz_val.astype(jnp.float32))
        return (outputs, dx_val.astype(jnp.bfloat16), dw_val)
    outputs, dx_all, dw_all = lax.map(one_group, (clips.reshape(groups, 4, SF + 2, H, W, C), cots.reshape(groups, 4, SF, H, W, C), lengths.reshape(groups, 4)))
    outputs = outputs.reshape(N_DP, 2, SF, H, W, C)
    stay_out = outputs[:, 0]
    guest_out = outputs[:, 1][mates]
    slab_grad = dx_all.reshape(NSLAB, SF + 2, H, W, C)
    weight_grad = lax.optimization_barrier(jnp.sum(dw_all, axis=0)) / math.sqrt(NSLAB * SF * H * W)
    return (stay_out, guest_out, slab_grad, weight_grad)
```

```python
import functools
import math

import jax
import jax.numpy as jnp
from jax import lax
from jax.experimental import pallas as pl
from jax.experimental.pallas import tpu as pltpu
from jax.sharding import Mesh
from jax.sharding import PartitionSpec as P

BF = jnp.bfloat16
F32 = jnp.float32
TAPS = 27
PADDED_TAPS = 32


def shifted_columns(rows, width):
    count = rows.shape[0]
    column = lax.broadcasted_iota(jnp.int32, rows.shape, 0) % width
    before = jnp.where(column == 0, 0.0, pltpu.roll(rows, 1, 0))
    after = jnp.where(column == width - 1, 0.0, pltpu.roll(rows, count - 1, 0))
    return before, after


def forward_kernel(lengths, core, clips, low, high, kernel, cot_stay, cot_guest,
                   y_stay, y_guest, dz_out, dz_first, dz_last, mine, other, wide, sums):
    slabs, frames, rows, width, chans = clips.shape
    out_frames = frames - 2
    x = jnp.concatenate([low[...], clips[...], high[...]], axis=2).reshape(-1, chans)
    shape = (slabs, frames, rows + 2, width, chans)
    before, after = shifted_columns(x.astype(F32), width)
    wide[:, :, :, :, 0:chans] = before.astype(BF).reshape(shape)
    wide[:, :, :, :, chans : 2 * chans] = x.reshape(shape)
    wide[:, :, :, :, 2 * chans :] = after.astype(BF).reshape(shape)
    places = slabs * out_frames * rows * width

    def window(tap_t, tap_h):
        return wide[:, tap_t : tap_t + out_frames, tap_h : tap_h + rows].reshape(places, 3 * chans)

    z = jnp.zeros((places, chans), F32)
    for tap in range(9):
        z = z + jnp.dot(window(tap // 3, tap % 3), kernel[tap], preferred_element_type=F32)
    sig = 1.0 / (1.0 + jnp.exp(-z))
    per = rows * width
    y = z * sig
    slope = sig * (1.0 + z * (1.0 - sig))
    parts = []
    for slab, (cot, out) in enumerate(((cot_stay, y_stay), (cot_guest, y_guest))):
        for frame in range(out_frames):
            valid = jnp.where(lengths[slab] > frame, 1.0, 0.0)
            at = (slab * out_frames + frame) * per
            out[frame] = (valid * y[at : at + per]).astype(BF).reshape(rows, width, chans)
            grad = cot[frame].reshape(per, chans).astype(F32)
            dz = (valid * grad * slope[at : at + per]).astype(BF)
            parts.append(dz)
            dz = dz.reshape(rows, width, chans)
            dz_out[slab, frame] = dz
            dz_first[slab, frame] = dz[0:1]
            dz_last[slab, frame] = dz[rows - 1 : rows]
    dz_all = jnp.concatenate(parts, axis=0)
    for tap in range(9):
        term = lax.dot_general(window(tap // 3, tap % 3), dz_all, (((0,), (0,)), ((), ())), preferred_element_type=F32)
        sums[3 * tap : 3 * tap + 3] = term.reshape(3, chans, chans)
    half = chans // 2
    own = core[0]
    mine[...] = sums[:, pl.ds(pl.multiple_of(own * half, half), half), :]
    other[...] = sums[:, pl.ds(pl.multiple_of((1 - own) * half, half), half), :].astype(BF)


def backward_kernel(dz, low, high, kernel, grads, wide):
    slabs, frames, rows, width, chans = dz.shape
    x = jnp.concatenate([low[...], dz[...], high[...]], axis=2).reshape(-1, chans)
    shape = (slabs, frames, rows + 2, width, chans)
    before, after = shifted_columns(x.astype(F32), width)
    wide[:, :, :, :, 0:chans] = after.astype(BF).reshape(shape)
    wide[:, :, :, :, chans : 2 * chans] = x.reshape(shape)
    wide[:, :, :, :, 2 * chans :] = before.astype(BF).reshape(shape)
    per = rows * width
    planes = []
    for tap_t in range(3):
        total = jnp.zeros((slabs * frames * per, chans), F32)
        for tap_h in range(3):
            rows_in = wide[:, :, 2 - tap_h : 2 - tap_h + rows].reshape(slabs * frames * per, 3 * chans)
            at = 3 * (3 * tap_t + tap_h)
            weights = jnp.concatenate([kernel[at], kernel[at + 1], kernel[at + 2]], axis=1)
            total = total + lax.dot_general(rows_in, weights, (((1,), (1,)), ((), ())), preferred_element_type=F32)
        planes.append(total)
    for slab in range(slabs):
        for frame in range(frames + 2):
            total = None
            for tap_t in range(3):
                source = frame - tap_t
                if 0 <= source < frames:
                    at = (slab * frames + source) * per
                    term = planes[tap_t][at : at + per]
                    total = term if total is None else total + term
            grads[slab, frame] = total.astype(BF).reshape(rows, width, chans)


def vmem(count):
    return [pl.BlockSpec(memory_space=pltpu.VMEM)] * count


def smem(count):
    return [pl.BlockSpec(memory_space=pltpu.SMEM)] * count


def forward_call(lengths, core, clips, low, high, kernel, cot_stay, cot_guest):
    slabs, frames, rows, width, chans = clips.shape
    out_frames = frames - 2
    one = (out_frames, rows, width, chans)
    edge = (slabs, out_frames, 1, width, chans)
    half = (TAPS, chans // 2, chans)
    return pl.pallas_call(
        forward_kernel,
        out_shape=(
            jax.ShapeDtypeStruct(one, BF),
            jax.ShapeDtypeStruct(one, BF),
            jax.ShapeDtypeStruct((slabs,) + one, BF),
            jax.ShapeDtypeStruct(edge, BF),
            jax.ShapeDtypeStruct(edge, BF),
            jax.ShapeDtypeStruct(half, F32),
            jax.ShapeDtypeStruct(half, BF),
        ),
        in_specs=smem(2) + vmem(6),
        out_specs=tuple(vmem(7)),
        scratch_shapes=[
            pltpu.VMEM((slabs, frames, rows + 2, width, 3 * chans), BF),
            pltpu.VMEM((TAPS, chans, chans), F32),
        ],
        compiler_params=pltpu.CompilerParams(vmem_limit_bytes=32 * 2**20),
        name="forward",
    )(lengths, core, clips, low, high, kernel, cot_stay, cot_guest)


def backward_call(dz, low, high, kernel):
    slabs, frames, rows, width, chans = dz.shape
    return pl.pallas_call(
        backward_kernel,
        out_shape=jax.ShapeDtypeStruct((slabs, frames + 2, rows, width, chans), BF),
        in_specs=vmem(4),
        out_specs=vmem(1)[0],
        scratch_shapes=[pltpu.VMEM((slabs, frames, rows + 2, width, 3 * chans), BF)],
        compiler_params=pltpu.CompilerParams(vmem_limit_bytes=32 * 2**20),
        name="backward",
    )(dz, low, high, kernel)


def by_xor(value, axes, count, offset):
    def branch(mask):
        pairs = [(source, source ^ mask) for source in range(count)]
        return lambda item: lax.ppermute(item, axes, pairs)

    return lax.switch(offset, [branch(mask) for mask in range(count)], value)


def route(value, offset, ny, nz):
    low = 2 * nz
    value = by_xor(value, ("z", "c"), low, jnp.bitwise_and(offset, low - 1))
    return by_xor(value, "y", ny, offset // low)


def swap_cores(value):
    return lax.ppermute(value, "c", [(0, 1), (1, 0)])


def spread(value, count):
    return jnp.broadcast_to(value[None], (count,) + value.shape)


def added(parts):
    return jnp.sum(parts.astype(F32), axis=0).astype(BF)


def summed(mine, other, scale, ny, nz, nx):
    core = lax.axis_index("c")
    half = mine + swap_cores(other).astype(F32)
    half = jnp.pad(half, ((0, PADDED_TAPS - TAPS), (0, 0), (0, 0))).astype(BF)
    held = half.shape
    parts = half.reshape((nz * nx, -1, held[2]))
    one = added(lax.all_to_all(parts, ("z", "x"), 0, 0))
    one = added(lax.all_to_all(spread(one, ny), "y", 0, 0))
    whole = lax.all_to_all(spread(one, nz * nx), ("z", "x"), 0, 0).reshape(held)
    theirs = swap_cores(whole)
    first = jnp.where(core == 0, whole, theirs)[:TAPS]
    second = jnp.where(core == 0, theirs, whole)[:TAPS]
    return jnp.concatenate([first, second], axis=1).astype(F32) * scale


def shards(ny, nz, nx, scale, clips, lengths, partner, kernel, cot_stay, cot_guest):
    rows = clips.shape[2]
    chans = clips.shape[4]
    offset = partner[0]
    up = [(i, i + 1) for i in range(nx - 1)]
    down = [(i + 1, i) for i in range(nx - 1)]

    def edges(first, last):
        return lax.ppermute(last, "x", up), lax.ppermute(first, "x", down)

    low, high = edges(clips[:, :, :1], clips[:, :, rows - 1 :])
    cot_here = route(cot_guest[0], offset, ny, nz)
    core = lax.axis_index("c").astype(jnp.int32).reshape(1)
    y_stay, y_guest, dz, dz_first, dz_last, mine, other = forward_call(
        lengths, core, clips, low, high, kernel.reshape(9, 3 * chans, chans), cot_stay[0], cot_here
    )
    dz_low, dz_high = edges(dz_first, dz_last)
    slab_grad = backward_call(dz, dz_low, dz_high, kernel.reshape(TAPS, chans, chans))
    guest_out = route(y_guest, offset, ny, nz)
    weight_grad = summed(mine, other, scale, ny, nz, nx).reshape(kernel.shape)
    return y_stay[None], guest_out[None], slab_grad, weight_grad


def solution(mesh):
    nx = mesh.shape["space"]
    ny = nz = math.isqrt(mesh.shape["dp"] // 2)
    fine = Mesh(mesh.devices.reshape(ny, nz, 2, nx), ("y", "z", "c", "x"))
    block = P(("y", "z", "c"), None, "x", None, None)

    def whole(clips, lengths, partner, kernel, cot_stay, cot_guest):
        slabs, _, height, width, _ = clips.shape
        scale = 1.0 / math.sqrt(slabs * cot_stay.shape[1] * height * width)
        return jax.shard_map(
            functools.partial(shards, ny, nz, nx, scale),
            mesh=fine,
            in_specs=(block, P(("y", "z", "c")), P(), P(), block, block),
            out_specs=(block, block, block, P()),
            check_vma=False,
        )(clips, lengths, partner, kernel, cot_stay, cot_guest)

    return whole
```

```python
import functools
import math

import jax
import jax.numpy as jnp
from jax import lax
from jax.experimental import pallas as pl
from jax.experimental.pallas import tpu as pltpu
from jax.sharding import Mesh
from jax.sharding import PartitionSpec as P

BF = jnp.bfloat16
F32 = jnp.float32
TAPS = 27
PADDED_TAPS = 32


def widen(wide, block, first, mirrored):
    slabs, frames, rows, width, chans = block.shape
    flat = block.reshape(-1, chans).astype(F32)
    column = lax.broadcasted_iota(jnp.int32, flat.shape, 0) % width
    before = jnp.where(column == 0, 0.0, pltpu.roll(flat, 1, 0)).astype(BF).reshape(block.shape)
    after = jnp.where(column == width - 1, 0.0, pltpu.roll(flat, flat.shape[0] - 1, 0)).astype(BF).reshape(block.shape)
    for part, columns in enumerate((after, block, before) if mirrored else (before, block, after)):
        wide[:, :, first : first + rows, :, part * chans : (part + 1) * chans] = columns


def forward_kernel(lengths, low, high, clips, kernel_in, y_stay, y_guest, slope_out, held, kernel, wide, sems):
    slabs, frames, rows, width, chans = clips.shape
    out_frames = frames - 2
    loads = [
        pltpu.make_async_copy(low, held.at[:, :, 0:1], sems.at[0]),
        pltpu.make_async_copy(clips, held.at[:, :, 1 : rows + 1], sems.at[1]),
        pltpu.make_async_copy(high, held.at[:, :, rows + 1 : rows + 2], sems.at[2]),
    ]
    weights = [
        pltpu.make_async_copy(kernel_in.at[3 * k : 3 * k + 3], kernel.at[3 * k : 3 * k + 3], sems.at[3 + k])
        for k in range(3)
    ]
    for load in loads + weights:
        load.start()
    for load in loads:
        load.wait()
    widen(wide, held[...], 0, False)
    places = slabs * out_frames * rows * width
    z = jnp.zeros((places, chans), F32)
    for tap in range(9):
        if tap % 3 == 0:
            weights[tap // 3].wait()
        z = z + jnp.dot(window(wide, tap, rows), kernel[tap], preferred_element_type=F32)
    sig = 1.0 / (1.0 + jnp.exp(-z))
    per = rows * width
    y = z * sig
    slope = sig * (1.0 + z * (1.0 - sig))
    for slab, out in enumerate((y_stay, y_guest)):
        for frame in range(out_frames):
            valid = jnp.where(lengths[slab] > frame, 1.0, 0.0)
            at = (slab * out_frames + frame) * per
            out[frame] = (valid * y[at : at + per]).astype(BF).reshape(rows, width, chans)
            slope_out[at : at + per] = valid * slope[at : at + per]


def window(wide, tap, rows):
    frames = wide.shape[1] - 2
    block = wide[:, tap // 3 : tap // 3 + frames, tap % 3 : tap % 3 + rows]
    return block.reshape(-1, wide.shape[4])


def weight_kernel(core, low, high, slope_in, cot_guest_in, clips, cot_stay,
                  dz_out, dz_first, dz_last, mine, other, edge, slope, cot_guest, wide, sums, sems):
    slabs, frames, rows, width, chans = clips.shape
    out_frames = frames - 2
    per = rows * width
    loads = [
        pltpu.make_async_copy(low, edge.at[0], sems.at[0]),
        pltpu.make_async_copy(high, edge.at[1], sems.at[1]),
        pltpu.make_async_copy(slope_in, slope, sems.at[2]),
        pltpu.make_async_copy(cot_guest_in, cot_guest, sems.at[3]),
    ]
    for load in loads:
        load.start()
    widen(wide, clips[...], 1, False)
    for load in loads:
        load.wait()
    for place in range(2):
        widen(wide, edge[place], place * (rows + 1), False)
    parts = []
    for slab, cot in enumerate((cot_stay, cot_guest)):
        for frame in range(out_frames):
            at = (slab * out_frames + frame) * per
            grad = cot[frame].reshape(per, chans).astype(F32)
            dz = (grad * slope[at : at + per]).astype(BF)
            parts.append(dz)
            dz = dz.reshape(rows, width, chans)
            dz_out[slab, frame] = dz
            dz_first[slab, frame] = dz[0:1]
            dz_last[slab, frame] = dz[rows - 1 : rows]
    dz_all = jnp.concatenate(parts, axis=0)
    for tap in range(9):
        term = lax.dot_general(
            window(wide, tap, rows), dz_all, (((0,), (0,)), ((), ())), preferred_element_type=F32
        )
        sums[3 * tap : 3 * tap + 3] = term.reshape(3, chans, chans)
    half = chans // 2
    own = core[0]
    mine[...] = sums[:, pl.ds(pl.multiple_of(own * half, half), half), :]
    other[...] = sums[:, pl.ds(pl.multiple_of((1 - own) * half, half), half), :].astype(BF)


def backward_kernel(dz, low, high, kernel, grads, wide):
    slabs, frames, rows, width, chans = dz.shape
    widen(wide, low[...], 0, True)
    widen(wide, dz[...], 1, True)
    widen(wide, high[...], rows + 1, True)
    per = rows * width
    planes = []
    for tap_t in range(3):
        total = jnp.zeros((slabs * frames * per, chans), F32)
        for tap_h in range(3):
            rows_in = wide[:, :, 2 - tap_h : 2 - tap_h + rows].reshape(slabs * frames * per, 3 * chans)
            at = 3 * (3 * tap_t + tap_h)
            weights = jnp.concatenate([kernel[at], kernel[at + 1], kernel[at + 2]], axis=1)
            total = total + lax.dot_general(rows_in, weights, (((1,), (1,)), ((), ())), preferred_element_type=F32)
        planes.append(total)
    for slab in range(slabs):
        for frame in range(frames + 2):
            total = None
            for tap_t in range(3):
                source = frame - tap_t
                if 0 <= source < frames:
                    at = (slab * frames + source) * per
                    term = planes[tap_t][at : at + per]
                    total = term if total is None else total + term
            grads[slab, frame] = total.astype(BF).reshape(rows, width, chans)


def vmem(count):
    return [pl.BlockSpec(memory_space=pltpu.VMEM)] * count


def smem(count):
    return [pl.BlockSpec(memory_space=pltpu.SMEM)] * count


def anywhere(count):
    return [pl.BlockSpec(memory_space=pl.ANY)] * count


def forward_call(lengths, low, high, clips, kernel):
    slabs, frames, rows, width, chans = clips.shape
    one = (frames - 2, rows, width, chans)
    return pl.pallas_call(
        forward_kernel,
        out_shape=(
            jax.ShapeDtypeStruct(one, BF),
            jax.ShapeDtypeStruct(one, BF),
            jax.ShapeDtypeStruct((slabs * (frames - 2) * rows * width, chans), F32),
        ),
        in_specs=smem(1) + anywhere(4),
        out_specs=tuple(vmem(3)),
        scratch_shapes=[
            pltpu.VMEM((slabs, frames, rows + 2, width, chans), BF),
            pltpu.VMEM(kernel.shape, BF),
            pltpu.VMEM((slabs, frames, rows + 2, width, 3 * chans), BF),
            pltpu.SemaphoreType.DMA((6,)),
        ],
        compiler_params=pltpu.CompilerParams(vmem_limit_bytes=32 * 2**20),
        name="forward",
    )(lengths, low, high, clips, kernel)


def weight_call(core, low, high, slope, cot_guest, clips, cot_stay):
    slabs, frames, rows, width, chans = clips.shape
    one = cot_stay.shape
    edge = (slabs, frames - 2, 1, width, chans)
    half = (TAPS, chans // 2, chans)
    return pl.pallas_call(
        weight_kernel,
        out_shape=(
            jax.ShapeDtypeStruct((slabs,) + one, BF),
            jax.ShapeDtypeStruct(edge, BF),
            jax.ShapeDtypeStruct(edge, BF),
            jax.ShapeDtypeStruct(half, F32),
            jax.ShapeDtypeStruct(half, BF),
        ),
        in_specs=smem(1) + anywhere(4) + vmem(2),
        out_specs=tuple(vmem(5)),
        scratch_shapes=[
            pltpu.VMEM((2,) + low.shape, BF),
            pltpu.VMEM(slope.shape, F32),
            pltpu.VMEM(one, BF),
            pltpu.VMEM((slabs, frames, rows + 2, width, 3 * chans), BF),
            pltpu.VMEM((TAPS, chans, chans), F32),
            pltpu.SemaphoreType.DMA((4,)),
        ],
        compiler_params=pltpu.CompilerParams(vmem_limit_bytes=32 * 2**20),
        name="weights",
    )(core, low, high, slope, cot_guest, clips, cot_stay)


def backward_call(dz, low, high, kernel):
    slabs, frames, rows, width, chans = dz.shape
    return pl.pallas_call(
        backward_kernel,
        out_shape=jax.ShapeDtypeStruct((slabs, frames + 2, rows, width, chans), BF),
        in_specs=vmem(4),
        out_specs=vmem(1)[0],
        scratch_shapes=[pltpu.VMEM((slabs, frames, rows + 2, width, 3 * chans), BF)],
        compiler_params=pltpu.CompilerParams(vmem_limit_bytes=32 * 2**20),
        name="backward",
    )(dz, low, high, kernel)


def half_kernel(scale, groups, first, rows, passed, out, passed_out, buffer, held, sems):
    taps, half, _ = buffer.shape
    step = taps // groups
    place = pl.ds(pl.multiple_of(first[0] * half, half), half)
    load = pltpu.make_async_copy(passed, held, sems.at[groups])
    load.start()
    copies = [pltpu.make_async_copy(held, passed_out.at[0], sems.at[groups + 1])]
    for group in range(groups):
        at = slice(group * step, group * step + step)
        buffer[at] = rows[at].astype(F32) * scale
        copies.append(pltpu.make_async_copy(buffer.at[at], out.at[at, place, :], sems.at[group]))
        copies[-1].start()
    load.wait()
    copies[0].start()
    for copy in copies:
        copy.wait()


def half_call(first, rows, scale, passed):
    _, half, chans = rows.shape
    return pl.pallas_call(
        functools.partial(half_kernel, scale, 3),
        out_shape=(
            jax.ShapeDtypeStruct((TAPS, 2 * half, chans), F32),
            jax.ShapeDtypeStruct((1,) + passed.shape, passed.dtype),
        ),
        in_specs=smem(1) + vmem(1) + anywhere(1),
        out_specs=tuple(anywhere(2)),
        scratch_shapes=[
            pltpu.VMEM((TAPS, half, chans), F32),
            pltpu.VMEM(passed.shape, passed.dtype),
            pltpu.SemaphoreType.DMA((5,)),
        ],
        compiler_params=pltpu.CompilerParams(vmem_limit_bytes=32 * 2**20),
        name="own",
    )(first, rows, passed)


def rest_kernel(scale, groups, first, rows, _, out, buffer, sems):
    taps, half, _ = buffer.shape
    step = taps // groups
    place = pl.ds(pl.multiple_of(first[0] * half, half), half)
    copies = []
    for group in range(groups):
        at = slice(group * step, group * step + step)
        buffer[at] = rows[at].astype(F32) * scale
        copies.append(pltpu.make_async_copy(buffer.at[at], out.at[at, place, :], sems.at[group]))
        copies[-1].start()
    for copy in copies:
        copy.wait()


def rest_call(first, rows, scale, earlier):
    _, half, chans = rows.shape
    return pl.pallas_call(
        functools.partial(rest_kernel, scale, 3),
        out_shape=jax.ShapeDtypeStruct(earlier.shape, F32),
        in_specs=smem(1) + vmem(1) + anywhere(1),
        out_specs=anywhere(1)[0],
        scratch_shapes=[pltpu.VMEM((TAPS, half, chans), F32), pltpu.SemaphoreType.DMA((3,))],
        input_output_aliases={2: 0},
        compiler_params=pltpu.CompilerParams(vmem_limit_bytes=32 * 2**20),
        name="rest",
    )(first, rows, earlier)


def by_xor(value, axes, count, offset, beside=None, extra=()):
    def branch(mask):
        pairs = [(source, source ^ mask) for source in range(count)]

        def moved(item, *others):
            there = lax.ppermute(item, axes, pairs)
            return there if beside is None else (there, beside(*others))

        return moved

    return lax.switch(offset, [branch(mask) for mask in range(count)], value, *extra)


def swap_cores(value):
    return lax.ppermute(value, "c", [(0, 1), (1, 0)])


def spread(value, count):
    return jnp.broadcast_to(value[None], (count,) + value.shape)


def added(parts):
    return jnp.sum(parts.astype(F32), axis=0).astype(BF)


def shards(ny, nz, nx, scale, clips, lengths, partner, kernel, cot_stay, cot_guest):
    rows = clips.shape[2]
    chans = clips.shape[4]
    near, far = jnp.bitwise_and(partner[0], 2 * nz - 1), partner[0] // (2 * nz)
    up = [(i, i + 1) for i in range(nx - 1)]
    down = [(i + 1, i) for i in range(nx - 1)]

    def edges(first, last):
        return lax.ppermute(last, "x", up), lax.ppermute(first, "x", down)

    def clip_edges(whole):
        return edges(whole[:, :, :1], whole[:, :, rows - 1 :])

    core = lax.axis_index("c").astype(jnp.int32).reshape(1)
    cot_here, (low, high) = by_xor(cot_guest[0], ("z", "c"), 2 * nz, near, clip_edges, (clips,))
    cot_here, (y_stay, y_guest, slope) = by_xor(
        cot_here, "y", ny, far, forward_call, (lengths, low, high, clips, kernel.reshape(9, 3 * chans, chans))
    )
    dz, dz_first, dz_last, mine, other = weight_call(core, low, high, slope, cot_here, clips, cot_stay[0])
    half = mine + swap_cores(other).astype(F32)
    half = jnp.pad(half, ((0, PADDED_TAPS - TAPS), (0, 0), (0, 0))).astype(BF)
    held = half.shape
    parts = lax.all_to_all(half.reshape((nz * nx, -1, held[2])), ("z", "x"), 0, 0)

    guest, (dz_low, dz_high) = by_xor(y_guest, "y", ny, far, edges, (dz_first, dz_last))
    one, guest, dz_low, dz_high = lax.optimization_barrier((added(parts), guest, dz_low, dz_high))
    parts = lax.all_to_all(spread(one, ny), "y", 0, 0)
    slab_grad = backward_call(dz, dz_low, dz_high, kernel.reshape(TAPS, chans, chans))
    one, slab_grad = lax.optimization_barrier((added(parts), slab_grad))
    whole = lax.all_to_all(spread(one, nz * nx), ("z", "x"), 0, 0).reshape(held)
    guest = by_xor(guest, ("z", "c"), 2 * nz, near)
    whole, guest = lax.optimization_barrier((whole, guest))
    theirs = swap_cores(whole)
    weight_grad, guest = half_call(core, whole, scale, guest)
    weight_grad = rest_call(1 - core, theirs, scale, weight_grad).reshape(kernel.shape)
    return y_stay[None], guest, slab_grad, weight_grad


def solution(mesh):
    nx = mesh.shape["space"]
    ny = nz = math.isqrt(mesh.shape["dp"] // 2)
    fine = Mesh(mesh.devices.reshape(ny, nz, 2, nx), ("y", "z", "c", "x"))
    block = P(("y", "z", "c"), None, "x", None, None)

    def whole(clips, lengths, partner, kernel, cot_stay, cot_guest):
        slabs, _, height, width, _ = clips.shape
        scale = 1.0 / math.sqrt(slabs * cot_stay.shape[1] * height * width)
        return jax.shard_map(
            functools.partial(shards, ny, nz, nx, scale),
            mesh=fine,
            in_specs=(block, P(("y", "z", "c")), P(), P(), block, block),
            out_specs=(block, block, block, P()),
            check_vma=False,
        )(clips, lengths, partner, kernel, cot_stay, cot_guest)

    return whole
```

```python
import functools
import math

import jax
import jax.numpy as jnp
from jax import lax
from jax.experimental import pallas as pl
from jax.experimental.pallas import tpu as pltpu
from jax.sharding import Mesh
from jax.sharding import PartitionSpec as P

BF = jnp.bfloat16
F32 = jnp.float32
TAPS = 27
HALF_TAPS = 14


def widen(wide, block, first, mirrored):
    slabs, frames, rows, width, chans = block.shape
    flat = block.reshape(-1, chans).astype(F32)
    column = lax.broadcasted_iota(jnp.int32, flat.shape, 0) % width
    before = jnp.where(column == 0, 0.0, pltpu.roll(flat, 1, 0)).astype(BF).reshape(block.shape)
    after = jnp.where(column == width - 1, 0.0, pltpu.roll(flat, flat.shape[0] - 1, 0)).astype(BF).reshape(block.shape)
    for part, columns in enumerate((after, block, before) if mirrored else (before, block, after)):
        wide[:, :, first : first + rows, :, part * chans : (part + 1) * chans] = columns


def forward_kernel(lengths, low, high, clips, kernel_in, y_stay, y_guest, slope_out, held, kernel, wide, sems):
    slabs, frames, rows, width, chans = clips.shape
    out_frames = frames - 2
    loads = [
        pltpu.make_async_copy(low, held.at[:, :, 0:1], sems.at[0]),
        pltpu.make_async_copy(clips, held.at[:, :, 1 : rows + 1], sems.at[1]),
        pltpu.make_async_copy(high, held.at[:, :, rows + 1 : rows + 2], sems.at[2]),
    ]
    weights = [
        pltpu.make_async_copy(kernel_in.at[3 * k : 3 * k + 3], kernel.at[3 * k : 3 * k + 3], sems.at[3 + k])
        for k in range(3)
    ]
    for load in loads + weights:
        load.start()
    for load in loads:
        load.wait()
    widen(wide, held[...], 0, False)
    places = slabs * out_frames * rows * width
    z = jnp.zeros((places, chans), F32)
    for tap in range(9):
        if tap % 3 == 0:
            weights[tap // 3].wait()
        z = z + jnp.dot(window(wide, tap, rows), kernel[tap], preferred_element_type=F32)
    sig = 1.0 / (1.0 + jnp.exp(-z))
    per = rows * width
    y = z * sig
    slope = sig * (1.0 + z * (1.0 - sig))
    for slab, out in enumerate((y_stay, y_guest)):
        for frame in range(out_frames):
            valid = jnp.where(lengths[slab] > frame, 1.0, 0.0)
            at = (slab * out_frames + frame) * per
            out[frame] = (valid * y[at : at + per]).astype(BF).reshape(rows, width, chans)
            slope_out[at : at + per] = valid * slope[at : at + per]


def window(wide, tap, rows):
    frames = wide.shape[1] - 2
    block = wide[:, tap // 3 : tap // 3 + frames, tap % 3 : tap % 3 + rows]
    return block.reshape(-1, wide.shape[4])


def half_weights(half, wide, turned, sums, rows):
    chans = turned.shape[0]
    first = 4 * half
    blocks = []
    for number in range(5):
        offset = first + number
        tap_t = lax.div(offset, 3)
        block = wide[:, pl.ds(tap_t, wide.shape[1] - 2), pl.ds(offset - 3 * tap_t, rows)]
        blocks.append(block.reshape(-1, wide.shape[4]))
    total = jnp.dot(turned[...], jnp.concatenate(blocks, axis=1), preferred_element_type=F32)
    for tap in range(15):
        sums[tap] = total[:, tap * chans : (tap + 1) * chans].T
    sums[15] = jnp.zeros((chans, chans), F32)
    return sums[pl.ds(2 * half, HALF_TAPS)]


def weight_kernel(core, low, high, slope_in, cot_guest_in, clips, cot_stay,
                  dz_out, dz_first, dz_last, other, wide, turned, edge, slope, cot_guest, sums, sems):
    slabs, frames, rows, width, chans = clips.shape
    out_frames = frames - 2
    per = rows * width
    loads = [
        pltpu.make_async_copy(low, edge.at[0], sems.at[0]),
        pltpu.make_async_copy(high, edge.at[1], sems.at[1]),
        pltpu.make_async_copy(slope_in, slope, sems.at[2]),
        pltpu.make_async_copy(cot_guest_in, cot_guest, sems.at[3]),
    ]
    for load in loads:
        load.start()
    widen(wide, clips[...], 1, False)
    for load in loads:
        load.wait()
    for place in range(2):
        widen(wide, edge[place], place * (rows + 1), False)
    parts = []
    for slab, cot in enumerate((cot_stay, cot_guest)):
        for frame in range(out_frames):
            at = (slab * out_frames + frame) * per
            grad = cot[frame].reshape(per, chans).astype(F32)
            dz = (grad * slope[at : at + per]).astype(BF)
            parts.append(dz)
            dz = dz.reshape(rows, width, chans)
            dz_out[slab, frame] = dz
            dz_first[slab, frame] = dz[0:1]
            dz_last[slab, frame] = dz[rows - 1 : rows]
    turned[...] = jnp.concatenate(parts, axis=0).astype(F32).T.astype(BF)
    other[...] = half_weights(1 - core[0], wide, turned, sums, rows).astype(BF)


def mine_kernel(core, wide, turned, mine, sums):
    mine[...] = half_weights(core[0], wide, turned, sums, wide.shape[2] - 2)


def joined_kernel(mine, got, out, buffer, sems):
    step = buffer.shape[0] // 2
    copies = []
    for part in range(2):
        at = slice(part * step, part * step + step)
        buffer[at] = (mine[at] + got[at].astype(F32)).astype(BF)
        copies.append(pltpu.make_async_copy(buffer.at[at], out.at[at], sems.at[part]))
        copies[-1].start()
    for copy in copies:
        copy.wait()


def spread_kernel(parts, out, buffer, sems):
    held, count = buffer.shape[0], out.shape[0]
    total = parts[0].astype(F32)
    for part in range(1, parts.shape[0]):
        total = total + parts[part].astype(F32)
    total = total.astype(BF)
    for place in range(held):
        buffer[place] = total
    copies = [
        pltpu.make_async_copy(buffer, out.at[first : first + held], sems.at[first // held])
        for first in range(0, count, held)
    ]
    for copy in copies:
        copy.start()
    for copy in copies:
        copy.wait()


def backward_kernel(dz, low, high, kernel, grads, wide):
    slabs, frames, rows, width, chans = dz.shape
    widen(wide, low[...], 0, True)
    widen(wide, dz[...], 1, True)
    widen(wide, high[...], rows + 1, True)
    per = rows * width
    planes = []
    for tap_t in range(3):
        total = jnp.zeros((slabs * frames * per, chans), F32)
        for tap_h in range(3):
            rows_in = wide[:, :, 2 - tap_h : 2 - tap_h + rows].reshape(slabs * frames * per, 3 * chans)
            at = 3 * (3 * tap_t + tap_h)
            weights = jnp.concatenate([kernel[at], kernel[at + 1], kernel[at + 2]], axis=1)
            total = total + lax.dot_general(rows_in, weights, (((1,), (1,)), ((), ())), preferred_element_type=F32)
        planes.append(total)
    for slab in range(slabs):
        for frame in range(frames + 2):
            total = None
            for tap_t in range(3):
                source = frame - tap_t
                if 0 <= source < frames:
                    at = (slab * frames + source) * per
                    term = planes[tap_t][at : at + per]
                    total = term if total is None else total + term
            grads[slab, frame] = total.astype(BF).reshape(rows, width, chans)


def vmem(count):
    return [pl.BlockSpec(memory_space=pltpu.VMEM)] * count


def smem(count):
    return [pl.BlockSpec(memory_space=pltpu.SMEM)] * count


def anywhere(count):
    return [pl.BlockSpec(memory_space=pl.ANY)] * count


def forward_call(lengths, low, high, clips, kernel):
    slabs, frames, rows, width, chans = clips.shape
    one = (frames - 2, rows, width, chans)
    return pl.pallas_call(
        forward_kernel,
        out_shape=(
            jax.ShapeDtypeStruct(one, BF),
            jax.ShapeDtypeStruct(one, BF),
            jax.ShapeDtypeStruct((slabs * (frames - 2) * rows * width, chans), F32),
        ),
        in_specs=smem(1) + anywhere(4),
        out_specs=tuple(vmem(3)),
        scratch_shapes=[
            pltpu.VMEM((slabs, frames, rows + 2, width, chans), BF),
            pltpu.VMEM(kernel.shape, BF),
            pltpu.VMEM((slabs, frames, rows + 2, width, 3 * chans), BF),
            pltpu.SemaphoreType.DMA((6,)),
        ],
        compiler_params=pltpu.CompilerParams(vmem_limit_bytes=32 * 2**20),
        name="forward",
    )(lengths, low, high, clips, kernel)


def weight_call(core, low, high, slope, cot_guest, clips, cot_stay):
    slabs, frames, rows, width, chans = clips.shape
    one = cot_stay.shape
    edge = (slabs, frames - 2, 1, width, chans)
    places = slabs * (frames - 2) * rows * width
    return pl.pallas_call(
        weight_kernel,
        out_shape=(
            jax.ShapeDtypeStruct((slabs,) + one, BF),
            jax.ShapeDtypeStruct(edge, BF),
            jax.ShapeDtypeStruct(edge, BF),
            jax.ShapeDtypeStruct((HALF_TAPS, chans, chans), BF),
            jax.ShapeDtypeStruct((slabs, frames, rows + 2, width, 3 * chans), BF),
            jax.ShapeDtypeStruct((chans, places), BF),
        ),
        in_specs=smem(1) + anywhere(4) + vmem(2),
        out_specs=tuple(vmem(6)),
        scratch_shapes=[
            pltpu.VMEM((2,) + low.shape, BF),
            pltpu.VMEM(slope.shape, F32),
            pltpu.VMEM(one, BF),
            pltpu.VMEM((16, chans, chans), F32),
            pltpu.SemaphoreType.DMA((4,)),
        ],
        compiler_params=pltpu.CompilerParams(vmem_limit_bytes=32 * 2**20),
        name="weights",
    )(core, low, high, slope, cot_guest, clips, cot_stay)


def mine_call(core, wide, turned):
    chans = turned.shape[0]
    return pl.pallas_call(
        mine_kernel,
        out_shape=jax.ShapeDtypeStruct((HALF_TAPS, chans, chans), F32),
        in_specs=smem(1) + vmem(2),
        out_specs=vmem(1)[0],
        scratch_shapes=[pltpu.VMEM((16, chans, chans), F32)],
        compiler_params=pltpu.CompilerParams(vmem_limit_bytes=32 * 2**20),
        name="mine",
    )(core, wide, turned)


def joined_call(mine, got):
    return pl.pallas_call(
        joined_kernel,
        out_shape=jax.ShapeDtypeStruct(mine.shape, BF),
        in_specs=vmem(2),
        out_specs=anywhere(1)[0],
        scratch_shapes=[pltpu.VMEM(mine.shape, BF), pltpu.SemaphoreType.DMA((2,))],
        compiler_params=pltpu.CompilerParams(vmem_limit_bytes=32 * 2**20),
        name="joined",
    )(mine, got)


def spread_call(parts, count):
    held = min(8, count)
    return pl.pallas_call(
        spread_kernel,
        out_shape=jax.ShapeDtypeStruct((count,) + parts.shape[1:], BF),
        in_specs=vmem(1),
        out_specs=anywhere(1)[0],
        scratch_shapes=[
            pltpu.VMEM((held,) + parts.shape[1:], BF),
            pltpu.SemaphoreType.DMA((count // held,)),
        ],
        compiler_params=pltpu.CompilerParams(vmem_limit_bytes=32 * 2**20),
        name="spread",
    )(parts)


def backward_call(dz, low, high, kernel):
    slabs, frames, rows, width, chans = dz.shape
    return pl.pallas_call(
        backward_kernel,
        out_shape=jax.ShapeDtypeStruct((slabs, frames + 2, rows, width, chans), BF),
        in_specs=vmem(4),
        out_specs=vmem(1)[0],
        scratch_shapes=[pltpu.VMEM((slabs, frames, rows + 2, width, 3 * chans), BF)],
        compiler_params=pltpu.CompilerParams(vmem_limit_bytes=32 * 2**20),
        name="backward",
    )(dz, low, high, kernel)


def write_taps(scale, first, rows, out, buffer, sems):
    pieces = ((0, 7), (7, HALF_TAPS - 1), (HALF_TAPS - 1, HALF_TAPS))
    copies = []
    for number, (low, high) in enumerate(pieces):
        buffer[low:high] = rows[low:high].astype(F32) * scale
        place = pl.ds(first[0] * HALF_TAPS + low, high - low)
        copies.append(pltpu.make_async_copy(buffer.at[low:high], out.at[place], sems.at[number]))
        if number < 2:
            copies[-1].start()
        else:
            pl.when(first[0] == 0)(copies[-1].start)

    def wait():
        copies[0].wait()
        copies[1].wait()
        pl.when(first[0] == 0)(copies[2].wait)

    return wait


def half_kernel(scale, first, rows, passed, out, passed_out, buffer, held, sems):
    load = pltpu.make_async_copy(passed, held, sems.at[3])
    store = pltpu.make_async_copy(held, passed_out.at[0], sems.at[4])
    load.start()
    wait = write_taps(scale, first, rows, out, buffer, sems)
    load.wait()
    store.start()
    wait()
    store.wait()


def half_call(first, rows, scale, passed):
    return pl.pallas_call(
        functools.partial(half_kernel, scale),
        out_shape=(
            jax.ShapeDtypeStruct((TAPS,) + rows.shape[1:], F32),
            jax.ShapeDtypeStruct((1,) + passed.shape, passed.dtype),
        ),
        in_specs=smem(1) + vmem(1) + anywhere(1),
        out_specs=tuple(anywhere(2)),
        scratch_shapes=[
            pltpu.VMEM(rows.shape, F32),
            pltpu.VMEM(passed.shape, passed.dtype),
            pltpu.SemaphoreType.DMA((5,)),
        ],
        compiler_params=pltpu.CompilerParams(vmem_limit_bytes=32 * 2**20),
        name="own",
    )(first, rows, passed)


def rest_kernel(scale, first, rows, _, out, buffer, sems):
    write_taps(scale, first, rows, out, buffer, sems)()


def rest_call(first, rows, scale, earlier):
    return pl.pallas_call(
        functools.partial(rest_kernel, scale),
        out_shape=jax.ShapeDtypeStruct(earlier.shape, F32),
        in_specs=smem(1) + vmem(1) + anywhere(1),
        out_specs=anywhere(1)[0],
        scratch_shapes=[pltpu.VMEM(rows.shape, F32), pltpu.SemaphoreType.DMA((3,))],
        input_output_aliases={2: 0},
        compiler_params=pltpu.CompilerParams(vmem_limit_bytes=32 * 2**20),
        name="rest",
    )(first, rows, earlier)


def by_xor(value, axes, count, offset, beside=None, extra=()):
    def branch(mask):
        pairs = [(source, source ^ mask) for source in range(count)]

        def moved(item, *others):
            there = lax.ppermute(item, axes, pairs)
            return there if beside is None else (there, beside(*others))

        return moved

    return lax.switch(offset, [branch(mask) for mask in range(count)], value, *extra)


def swap_cores(value):
    return lax.ppermute(value, "c", [(0, 1), (1, 0)])


def shards(ny, nz, nx, scale, clips, lengths, partner, kernel, cot_stay, cot_guest):
    rows = clips.shape[2]
    chans = clips.shape[4]
    near = jnp.bitwise_and(partner[0], 2 * nz - 1)
    far = lax.shift_right_logical(partner[0], jnp.int32((2 * nz).bit_length() - 1))
    up = [(i, i + 1) for i in range(nx - 1)]
    down = [(i + 1, i) for i in range(nx - 1)]

    def edges(first, last):
        return lax.ppermute(last, "x", up), lax.ppermute(first, "x", down)

    core = lax.axis_index("c").astype(jnp.int32).reshape(1)
    first, last = lax.optimization_barrier((clips[:, :, :1], clips[:, :, rows - 1 :]))
    cot_here, (low, high) = by_xor(cot_guest[0], ("z", "c"), 2 * nz, near, edges, (first, last))
    cot_here, (y_stay, y_guest, slope) = by_xor(
        cot_here, "y", ny, far, forward_call, (lengths, low, high, clips, kernel.reshape(9, 3 * chans, chans))
    )
    dz, dz_first, dz_last, other, wide, turned = weight_call(core, low, high, slope, cot_here, clips, cot_stay[0])
    half = joined_call(mine_call(core, wide, turned), swap_cores(other))
    parts = lax.all_to_all(half.reshape(ny * nx, -1, chans), ("y", "x"), 0, 0)
    guest, (dz_low, dz_high) = by_xor(y_guest, "y", ny, far, edges, (dz_first, dz_last))
    parts, guest, dz_low, dz_high = lax.optimization_barrier((parts, guest, dz_low, dz_high))
    parts = lax.all_to_all(spread_call(parts, nz), "z", 0, 0)
    slab_grad = backward_call(dz, dz_low, dz_high, kernel.reshape(TAPS, chans, chans))
    parts, slab_grad = lax.optimization_barrier((parts, slab_grad))
    whole = lax.all_to_all(spread_call(parts, ny * nx), ("y", "x"), 0, 0).reshape(half.shape)
    guest = by_xor(guest, ("z", "c"), 2 * nz, near)
    whole, guest = lax.optimization_barrier((whole, guest))
    theirs = swap_cores(whole)
    weight_grad, guest = half_call(core, whole, scale, guest)
    weight_grad = rest_call(1 - core, theirs, scale, weight_grad).reshape(kernel.shape)
    return y_stay[None], guest, slab_grad, weight_grad


def solution(mesh):
    nx = mesh.shape["space"]
    ny = nz = math.isqrt(mesh.shape["dp"] // 2)
    fine = Mesh(mesh.devices.reshape(ny, nz, 2, nx), ("y", "z", "c", "x"))
    block = P(("y", "z", "c"), None, "x", None, None)

    def whole(clips, lengths, partner, kernel, cot_stay, cot_guest):
        slabs, _, height, width, _ = clips.shape
        scale = 1.0 / math.sqrt(slabs * cot_stay.shape[1] * height * width)
        return jax.shard_map(
            functools.partial(shards, ny, nz, nx, scale),
            mesh=fine,
            in_specs=(block, P(("y", "z", "c")), P(), P(), block, block),
            out_specs=(block, block, block, P()),
            check_vma=False,
        )(clips, lengths, partner, kernel, cot_stay, cot_guest)

    return whole
```

```python
import functools
import math

import jax
import jax.numpy as jnp
from jax import lax
from jax.experimental import pallas as pl
from jax.experimental.pallas import tpu as pltpu
from jax.sharding import Mesh
from jax.sharding import PartitionSpec as P

BF = jnp.bfloat16
F32 = jnp.float32
TAPS = 27
HALF_TAPS = 14


def widen(wide, block, first, mirrored):
    slabs, frames, rows, width, chans = block.shape
    flat = block.reshape(-1, chans).astype(F32)
    column = lax.broadcasted_iota(jnp.int32, flat.shape, 0) % width
    before = jnp.where(column == 0, 0.0, pltpu.roll(flat, 1, 0)).astype(BF).reshape(block.shape)
    after = jnp.where(column == width - 1, 0.0, pltpu.roll(flat, flat.shape[0] - 1, 0)).astype(BF).reshape(block.shape)
    for part, columns in enumerate((after, block, before) if mirrored else (before, block, after)):
        wide[:, :, first : first + rows, :, part * chans : (part + 1) * chans] = columns


def forward_kernel(lengths, low, high, clips, kernel_in, y_stay, y_guest, slope_out, held, kernel, wide, sems):
    slabs, frames, rows, width, chans = clips.shape
    out_frames = frames - 2
    loads = [
        pltpu.make_async_copy(low, held.at[:, :, 0:1], sems.at[0]),
        pltpu.make_async_copy(clips, held.at[:, :, 1 : rows + 1], sems.at[1]),
        pltpu.make_async_copy(high, held.at[:, :, rows + 1 : rows + 2], sems.at[2]),
    ]
    weights = [
        pltpu.make_async_copy(kernel_in.at[3 * k : 3 * k + 3], kernel.at[3 * k : 3 * k + 3], sems.at[3 + k])
        for k in range(3)
    ]
    for load in loads + weights:
        load.start()
    for load in loads:
        load.wait()

    def widen_frame(number, carry):
        slab = lax.div(number, frames)
        at = (pl.ds(slab, 1), pl.ds(number - slab * frames, 1))
        widen(wide.at[at], held[at], 0, False)
        return carry

    lax.fori_loop(0, slabs * frames, widen_frame, 0)
    for load in weights:
        load.wait()
    windows = jnp.concatenate([window(wide, tap, rows) for tap in range(9)], axis=1)
    z = jnp.dot(windows, kernel[...].reshape(-1, chans), preferred_element_type=F32)
    sig = 1.0 / (1.0 + jnp.exp(-z))
    per = rows * width
    y = z * sig
    slope = sig * (1.0 + z * (1.0 - sig))
    for slab, out in enumerate((y_stay, y_guest)):
        for frame in range(out_frames):
            valid = jnp.where(lengths[slab] > frame, 1.0, 0.0)
            at = (slab * out_frames + frame) * per
            out[frame] = (valid * y[at : at + per]).astype(BF).reshape(rows, width, chans)
            slope_out[at : at + per] = valid * slope[at : at + per]


def window(wide, tap, rows):
    frames = wide.shape[1] - 2
    block = wide[:, tap // 3 : tap // 3 + frames, tap % 3 : tap % 3 + rows]
    return block.reshape(-1, wide.shape[4])


def half_weights(half, wide, turned, sums, rows):
    chans = turned.shape[0]
    first = 4 * half
    blocks = []
    for number in range(5):
        offset = first + number
        tap_t = lax.div(offset, 3)
        block = wide[:, pl.ds(tap_t, wide.shape[1] - 2), pl.ds(offset - 3 * tap_t, rows)]
        blocks.append(block.reshape(-1, wide.shape[4]))
    total = jnp.dot(turned[...], jnp.concatenate(blocks, axis=1), preferred_element_type=F32)
    for tap in range(15):
        sums[tap] = total[:, tap * chans : (tap + 1) * chans].T
    sums[15] = jnp.zeros((chans, chans), F32)
    return sums[pl.ds(2 * half, HALF_TAPS)]


def weight_kernel(core, low, high, slope_in, cot_guest_in, clips, cot_stay,
                  dz_out, dz_first, dz_last, other, wide, turned, edge, slope, cot_guest, sums, sems):
    slabs, frames, rows, width, chans = clips.shape
    out_frames = frames - 2
    per = rows * width
    loads = [
        pltpu.make_async_copy(low, edge.at[0], sems.at[0]),
        pltpu.make_async_copy(high, edge.at[1], sems.at[1]),
        pltpu.make_async_copy(slope_in, slope, sems.at[2]),
        pltpu.make_async_copy(cot_guest_in, cot_guest, sems.at[3]),
    ]
    for load in loads:
        load.start()
    widen(wide, clips[...], 1, False)
    for load in loads:
        load.wait()
    for place in range(2):
        widen(wide, edge[place], place * (rows + 1), False)
    parts = []
    for slab, cot in enumerate((cot_stay, cot_guest)):
        for frame in range(out_frames):
            at = (slab * out_frames + frame) * per
            grad = cot[frame].reshape(per, chans).astype(F32)
            dz = (grad * slope[at : at + per]).astype(BF)
            parts.append(dz)
            dz = dz.reshape(rows, width, chans)
            dz_out[slab, frame] = dz
            dz_first[slab, frame] = dz[0:1]
            dz_last[slab, frame] = dz[rows - 1 : rows]
    turned[...] = jnp.concatenate(parts, axis=0).astype(F32).T.astype(BF)
    other[...] = half_weights(1 - core[0], wide, turned, sums, rows).astype(BF)


def mine_kernel(core, wide, turned, mine, sums):
    mine[...] = half_weights(core[0], wide, turned, sums, wide.shape[2] - 2)


def joined_kernel(mine, got, out, buffer, sems):
    step = buffer.shape[0] // 2
    copies = []
    for part in range(2):
        at = slice(part * step, part * step + step)
        buffer[at] = (mine[at] + got[at].astype(F32)).astype(BF)
        copies.append(pltpu.make_async_copy(buffer.at[at], out.at[at], sems.at[part]))
        copies[-1].start()
    for copy in copies:
        copy.wait()


def spread_kernel(parts, out, buffer, sems):
    held, count = buffer.shape[0], out.shape[0]
    total = parts[0].astype(F32)
    for part in range(1, parts.shape[0]):
        total = total + parts[part].astype(F32)
    total = total.astype(BF)
    for place in range(held):
        buffer[place] = total
    copies = [
        pltpu.make_async_copy(buffer, out.at[first : first + held], sems.at[first // held])
        for first in range(0, count, held)
    ]
    for copy in copies:
        copy.start()
    for copy in copies:
        copy.wait()


def backward_kernel(dz, low, high, kernel, grads, wide):
    slabs, frames, rows, width, chans = dz.shape
    widen(wide, low[...], 0, True)
    widen(wide, dz[...], 1, True)
    widen(wide, high[...], rows + 1, True)
    per = rows * width
    planes = []
    for tap_t in range(3):
        total = jnp.zeros((slabs * frames * per, chans), F32)
        for tap_h in range(3):
            rows_in = wide[:, :, 2 - tap_h : 2 - tap_h + rows].reshape(slabs * frames * per, 3 * chans)
            at = 3 * (3 * tap_t + tap_h)
            weights = jnp.concatenate([kernel[at], kernel[at + 1], kernel[at + 2]], axis=1)
            total = total + lax.dot_general(rows_in, weights, (((1,), (1,)), ((), ())), preferred_element_type=F32)
        planes.append(total)
    for slab in range(slabs):
        for frame in range(frames + 2):
            total = None
            for tap_t in range(3):
                source = frame - tap_t
                if 0 <= source < frames:
                    at = (slab * frames + source) * per
                    term = planes[tap_t][at : at + per]
                    total = term if total is None else total + term
            grads[slab, frame] = total.astype(BF).reshape(rows, width, chans)


def vmem(count):
    return [pl.BlockSpec(memory_space=pltpu.VMEM)] * count


def smem(count):
    return [pl.BlockSpec(memory_space=pltpu.SMEM)] * count


def anywhere(count):
    return [pl.BlockSpec(memory_space=pl.ANY)] * count


def forward_call(lengths, low, high, clips, kernel):
    slabs, frames, rows, width, chans = clips.shape
    one = (frames - 2, rows, width, chans)
    return pl.pallas_call(
        forward_kernel,
        out_shape=(
            jax.ShapeDtypeStruct(one, BF),
            jax.ShapeDtypeStruct(one, BF),
            jax.ShapeDtypeStruct((slabs * (frames - 2) * rows * width, chans), F32),
        ),
        in_specs=smem(1) + anywhere(4),
        out_specs=tuple(vmem(3)),
        scratch_shapes=[
            pltpu.VMEM((slabs, frames, rows + 2, width, chans), BF),
            pltpu.VMEM(kernel.shape, BF),
            pltpu.VMEM((slabs, frames, rows + 2, width, 3 * chans), BF),
            pltpu.SemaphoreType.DMA((6,)),
        ],
        compiler_params=pltpu.CompilerParams(vmem_limit_bytes=32 * 2**20),
        name="forward",
    )(lengths, low, high, clips, kernel)


def weight_call(core, low, high, slope, cot_guest, clips, cot_stay):
    slabs, frames, rows, width, chans = clips.shape
    one = cot_stay.shape
    edge = (slabs, frames - 2, 1, width, chans)
    places = slabs * (frames - 2) * rows * width
    return pl.pallas_call(
        weight_kernel,
        out_shape=(
            jax.ShapeDtypeStruct((slabs,) + one, BF),
            jax.ShapeDtypeStruct(edge, BF),
            jax.ShapeDtypeStruct(edge, BF),
            jax.ShapeDtypeStruct((HALF_TAPS, chans, chans), BF),
            jax.ShapeDtypeStruct((slabs, frames, rows + 2, width, 3 * chans), BF),
            jax.ShapeDtypeStruct((chans, places), BF),
        ),
        in_specs=smem(1) + anywhere(4) + vmem(2),
        out_specs=tuple(vmem(6)),
        scratch_shapes=[
            pltpu.VMEM((2,) + low.shape, BF),
            pltpu.VMEM(slope.shape, F32),
            pltpu.VMEM(one, BF),
            pltpu.VMEM((16, chans, chans), F32),
            pltpu.SemaphoreType.DMA((4,)),
        ],
        compiler_params=pltpu.CompilerParams(vmem_limit_bytes=32 * 2**20),
        name="weights",
    )(core, low, high, slope, cot_guest, clips, cot_stay)


def mine_call(core, wide, turned):
    chans = turned.shape[0]
    return pl.pallas_call(
        mine_kernel,
        out_shape=jax.ShapeDtypeStruct((HALF_TAPS, chans, chans), F32),
        in_specs=smem(1) + vmem(2),
        out_specs=vmem(1)[0],
        scratch_shapes=[pltpu.VMEM((16, chans, chans), F32)],
        compiler_params=pltpu.CompilerParams(vmem_limit_bytes=32 * 2**20),
        name="mine",
    )(core, wide, turned)


def joined_call(mine, got):
    return pl.pallas_call(
        joined_kernel,
        out_shape=jax.ShapeDtypeStruct(mine.shape, BF),
        in_specs=vmem(2),
        out_specs=anywhere(1)[0],
        scratch_shapes=[pltpu.VMEM(mine.shape, BF), pltpu.SemaphoreType.DMA((2,))],
        compiler_params=pltpu.CompilerParams(vmem_limit_bytes=32 * 2**20),
        name="joined",
    )(mine, got)


def spread_call(parts, count):
    held = min(8, count)
    return pl.pallas_call(
        spread_kernel,
        out_shape=jax.ShapeDtypeStruct((count,) + parts.shape[1:], BF),
        in_specs=vmem(1),
        out_specs=anywhere(1)[0],
        scratch_shapes=[
            pltpu.VMEM((held,) + parts.shape[1:], BF),
            pltpu.SemaphoreType.DMA((count // held,)),
        ],
        compiler_params=pltpu.CompilerParams(vmem_limit_bytes=32 * 2**20),
        name="spread",
    )(parts)


def backward_call(dz, low, high, kernel):
    slabs, frames, rows, width, chans = dz.shape
    return pl.pallas_call(
        backward_kernel,
        out_shape=jax.ShapeDtypeStruct((slabs, frames + 2, rows, width, chans), BF),
        in_specs=vmem(4),
        out_specs=vmem(1)[0],
        scratch_shapes=[pltpu.VMEM((slabs, frames, rows + 2, width, 3 * chans), BF)],
        compiler_params=pltpu.CompilerParams(vmem_limit_bytes=32 * 2**20),
        name="backward",
    )(dz, low, high, kernel)


def write_taps(scale, first, rows, out, buffer, sems):
    pieces = ((0, 7), (7, HALF_TAPS - 1), (HALF_TAPS - 1, HALF_TAPS))
    copies = []
    for number, (low, high) in enumerate(pieces):
        buffer[low:high] = rows[low:high].astype(F32) * scale
        place = pl.ds(first[0] * HALF_TAPS + low, high - low)
        copies.append(pltpu.make_async_copy(buffer.at[low:high], out.at[place], sems.at[number]))
        if number < 2:
            copies[-1].start()
        else:
            pl.when(first[0] == 0)(copies[-1].start)

    def wait():
        copies[0].wait()
        copies[1].wait()
        pl.when(first[0] == 0)(copies[2].wait)

    return wait


def half_kernel(scale, first, rows, passed, out, passed_out, buffer, held, sems):
    load = pltpu.make_async_copy(passed, held, sems.at[3])
    store = pltpu.make_async_copy(held, passed_out.at[0], sems.at[4])
    load.start()
    wait = write_taps(scale, first, rows, out, buffer, sems)
    load.wait()
    store.start()
    wait()
    store.wait()


def half_call(first, rows, scale, passed):
    return pl.pallas_call(
        functools.partial(half_kernel, scale),
        out_shape=(
            jax.ShapeDtypeStruct((TAPS,) + rows.shape[1:], F32),
            jax.ShapeDtypeStruct((1,) + passed.shape, passed.dtype),
        ),
        in_specs=smem(1) + vmem(1) + anywhere(1),
        out_specs=tuple(anywhere(2)),
        scratch_shapes=[
            pltpu.VMEM(rows.shape, F32),
            pltpu.VMEM(passed.shape, passed.dtype),
            pltpu.SemaphoreType.DMA((5,)),
        ],
        compiler_params=pltpu.CompilerParams(vmem_limit_bytes=32 * 2**20),
        name="own",
    )(first, rows, passed)


def rest_kernel(scale, first, rows, _, out, buffer, sems):
    write_taps(scale, first, rows, out, buffer, sems)()


def rest_call(first, rows, scale, earlier):
    return pl.pallas_call(
        functools.partial(rest_kernel, scale),
        out_shape=jax.ShapeDtypeStruct(earlier.shape, F32),
        in_specs=smem(1) + vmem(1) + anywhere(1),
        out_specs=anywhere(1)[0],
        scratch_shapes=[pltpu.VMEM(rows.shape, F32), pltpu.SemaphoreType.DMA((3,))],
        input_output_aliases={2: 0},
        compiler_params=pltpu.CompilerParams(vmem_limit_bytes=32 * 2**20),
        name="rest",
    )(first, rows, earlier)


def ring_hops(count):
    table = 0
    for mask in range(count):
        hops = [min((i ^ mask) - i & count - 1, i - (i ^ mask) & count - 1) for i in range(count)]
        table |= (sum(hops) // count) << (4 * mask)
    return table


def hops_of(mask, table):
    return jnp.bitwise_and(lax.shift_right_logical(jnp.int32(table), 4 * mask), 15)


def masks_of(axes, count):
    return [(axes, count, mask) for mask in range(count)]


def by_xor(value, masks, place, beside=None, extra=()):
    def branch(axes, count, mask):
        pairs = [(source, source ^ mask) for source in range(count)]

        def moved(item, *others):
            there = lax.ppermute(item, axes, pairs)
            return there if beside is None else (there, beside(*others))

        return moved

    return lax.switch(place, [branch(*entry) for entry in masks], value, *extra)


def swap_cores(value):
    return lax.ppermute(value, "c", [(0, 1), (1, 0)])


def shards(ny, nz, nx, scale, clips, lengths, partner, kernel, cot_stay, cot_guest):
    rows = clips.shape[2]
    chans = clips.shape[4]
    near = jnp.bitwise_and(partner[0], 2 * nz - 1)
    far = lax.shift_right_logical(partner[0], jnp.int32((2 * nz).bit_length() - 1))
    near_masks, far_masks = masks_of(("z", "c"), 2 * nz), masks_of("y", ny)
    far_first = hops_of(far, ring_hops(ny)) > hops_of(lax.shift_right_logical(near, jnp.int32(1)), ring_hops(nz))
    one_way, other_way = near, 2 * nz + far
    first_way = jnp.where(far_first, other_way, one_way)
    second_way = jnp.where(far_first, one_way, other_way)
    up = [(i, i + 1) for i in range(nx - 1)]
    down = [(i + 1, i) for i in range(nx - 1)]

    def edges(first, last):
        return lax.ppermute(last, "x", up), lax.ppermute(first, "x", down)

    core = lax.axis_index("c").astype(jnp.int32).reshape(1)
    first, last = lax.optimization_barrier((clips[:, :, :1], clips[:, :, rows - 1 :]))
    cot_here, (low, high) = by_xor(cot_guest[0], near_masks + far_masks, first_way, edges, (first, last))
    weights = kernel.reshape(9, 3 * chans, chans)
    cot_here, (y_stay, y_guest, slope) = by_xor(
        cot_here, near_masks + far_masks, second_way, forward_call, (lengths, low, high, clips, weights)
    )
    dz, dz_first, dz_last, other, wide, turned = weight_call(core, low, high, slope, cot_here, clips, cot_stay[0])
    half = joined_call(mine_call(core, wide, turned), swap_cores(other))
    parts = lax.all_to_all(half.reshape(ny * nx, -1, chans), ("y", "x"), 0, 0)
    guest, (dz_low, dz_high) = by_xor(y_guest, far_masks, far, edges, (dz_first, dz_last))
    parts, guest, dz_low, dz_high = lax.optimization_barrier((parts, guest, dz_low, dz_high))
    parts = lax.all_to_all(spread_call(parts, nz), "z", 0, 0)
    slab_grad = backward_call(dz, dz_low, dz_high, kernel.reshape(TAPS, chans, chans))
    parts, slab_grad = lax.optimization_barrier((parts, slab_grad))
    whole = lax.all_to_all(spread_call(parts, ny * nx), ("y", "x"), 0, 0).reshape(half.shape)
    guest = by_xor(guest, near_masks, near)
    whole, guest = lax.optimization_barrier((whole, guest))
    theirs = swap_cores(whole)
    weight_grad, guest = half_call(core, whole, scale, guest)
    weight_grad = rest_call(1 - core, theirs, scale, weight_grad).reshape(kernel.shape)
    return y_stay[None], guest, slab_grad, weight_grad


def solution(mesh):
    nx = mesh.shape["space"]
    ny = nz = math.isqrt(mesh.shape["dp"] // 2)
    fine = Mesh(mesh.devices.reshape(ny, nz, 2, nx), ("y", "z", "c", "x"))
    block = P(("y", "z", "c"), None, "x", None, None)

    def whole(clips, lengths, partner, kernel, cot_stay, cot_guest):
        slabs, _, height, width, _ = clips.shape
        scale = 1.0 / math.sqrt(slabs * cot_stay.shape[1] * height * width)
        return jax.shard_map(
            functools.partial(shards, ny, nz, nx, scale),
            mesh=fine,
            in_specs=(block, P(("y", "z", "c")), P(), P(), block, block),
            out_specs=(block, block, block, P()),
            check_vma=False,
        )(clips, lengths, partner, kernel, cot_stay, cot_guest)

    return whole
```

```python
import functools
import math

import jax
import jax.numpy as jnp
from jax import lax
from jax.experimental import pallas as pl
from jax.experimental.pallas import tpu as pltpu
from jax.sharding import Mesh
from jax.sharding import PartitionSpec as P

BF = jnp.bfloat16
F32 = jnp.float32
TAPS = 27
HALF_TAPS = 14


def widen(wide, block, first, mirrored):
    slabs, frames, rows, width, chans = block.shape
    flat = block.reshape(-1, chans).astype(F32)
    column = lax.broadcasted_iota(jnp.int32, flat.shape, 0) % width
    before = jnp.where(column == 0, 0.0, pltpu.roll(flat, 1, 0)).astype(BF).reshape(block.shape)
    after = jnp.where(column == width - 1, 0.0, pltpu.roll(flat, flat.shape[0] - 1, 0)).astype(BF).reshape(block.shape)
    for part, columns in enumerate((after, block, before) if mirrored else (before, block, after)):
        wide[:, :, first : first + rows, :, part * chans : (part + 1) * chans] = columns


def forward_kernel(lengths, low, high, clips, kernel_in, y_stay, y_guest, slope_out, held, kernel, wide, sems):
    slabs, frames, rows, width, chans = clips.shape
    out_frames = frames - 2
    loads = [
        pltpu.make_async_copy(low, held.at[:, :, 0:1], sems.at[0]),
        pltpu.make_async_copy(clips, held.at[:, :, 1 : rows + 1], sems.at[1]),
        pltpu.make_async_copy(high, held.at[:, :, rows + 1 : rows + 2], sems.at[2]),
    ]
    weights = [
        pltpu.make_async_copy(kernel_in.at[3 * k : 3 * k + 3], kernel.at[3 * k : 3 * k + 3], sems.at[3 + k])
        for k in range(3)
    ]
    for load in loads + weights:
        load.start()
    for load in loads:
        load.wait()

    def widen_frame(number, carry):
        slab = lax.div(number, frames)
        at = (pl.ds(slab, 1), pl.ds(number - slab * frames, 1))
        widen(wide.at[at], held[at], 0, False)
        return carry

    lax.fori_loop(0, slabs * frames, widen_frame, 0)
    for load in weights:
        load.wait()
    windows = jnp.concatenate([window(wide, tap, rows) for tap in range(9)], axis=1)
    z = jnp.dot(windows, kernel[...].reshape(-1, chans), preferred_element_type=F32)
    sig = 1.0 / (1.0 + jnp.exp(-z))
    per = rows * width
    y = z * sig
    slope = sig * (1.0 + z * (1.0 - sig))
    for slab, out in enumerate((y_stay, y_guest)):
        for frame in range(out_frames):
            valid = jnp.where(lengths[slab] > frame, 1.0, 0.0)
            at = (slab * out_frames + frame) * per
            out[frame] = (valid * y[at : at + per]).astype(BF).reshape(rows, width, chans)
            slope_out[at : at + per] = valid * slope[at : at + per]


def window(wide, tap, rows):
    frames = wide.shape[1] - 2
    block = wide[:, tap // 3 : tap // 3 + frames, tap % 3 : tap % 3 + rows]
    return block.reshape(-1, wide.shape[4])


def half_weights(half, wide, turned, sums, rows):
    chans = turned.shape[0]
    first = 4 * half
    blocks = []
    for number in range(5):
        offset = first + number
        tap_t = lax.div(offset, 3)
        block = wide[:, pl.ds(tap_t, wide.shape[1] - 2), pl.ds(offset - 3 * tap_t, rows)]
        blocks.append(block.reshape(-1, wide.shape[4]))
    total = jnp.dot(turned[...], jnp.concatenate(blocks, axis=1), preferred_element_type=F32)
    for tap in range(15):
        sums[tap] = total[:, tap * chans : (tap + 1) * chans].T
    sums[15] = jnp.zeros((chans, chans), F32)
    return sums[pl.ds(2 * half, HALF_TAPS)]


def weight_kernel(core, low, high, slope_in, cot_guest_in, clips, cot_stay,
                  dz_out, dz_first, dz_last, other, wide, turned, edge, slope, cot_guest, sums, sems):
    slabs, frames, rows, width, chans = clips.shape
    out_frames = frames - 2
    per = rows * width
    loads = [
        pltpu.make_async_copy(low, edge.at[0], sems.at[0]),
        pltpu.make_async_copy(high, edge.at[1], sems.at[1]),
        pltpu.make_async_copy(slope_in, slope, sems.at[2]),
        pltpu.make_async_copy(cot_guest_in, cot_guest, sems.at[3]),
    ]
    for load in loads:
        load.start()
    widen(wide, clips[...], 1, False)
    for load in loads:
        load.wait()
    for place in range(2):
        widen(wide, edge[place], place * (rows + 1), False)
    parts = []
    for slab, cot in enumerate((cot_stay, cot_guest)):
        for frame in range(out_frames):
            at = (slab * out_frames + frame) * per
            grad = cot[frame].reshape(per, chans).astype(F32)
            dz = (grad * slope[at : at + per]).astype(BF)
            parts.append(dz)
            dz = dz.reshape(rows, width, chans)
            dz_out[slab, frame] = dz
            dz_first[slab, frame] = dz[0:1]
            dz_last[slab, frame] = dz[rows - 1 : rows]
    turned[...] = jnp.concatenate(parts, axis=0).astype(F32).T.astype(BF)
    other[...] = half_weights(1 - core[0], wide, turned, sums, rows).astype(BF)


def mine_kernel(core, wide, turned, mine, sums):
    mine[...] = half_weights(core[0], wide, turned, sums, wide.shape[2] - 2)


def joined_kernel(mine, got, out, buffer, sems):
    step = buffer.shape[0] // 2
    copies = []
    for part in range(2):
        at = slice(part * step, part * step + step)
        buffer[at] = (mine[at] + got[at].astype(F32)).astype(BF)
        copies.append(pltpu.make_async_copy(buffer.at[at], out.at[at], sems.at[part]))
        copies[-1].start()
    for copy in copies:
        copy.wait()


def spread_kernel(parts, out, buffer, sems):
    held, count = buffer.shape[0], out.shape[0]
    total = parts[0].astype(F32)
    for part in range(1, parts.shape[0]):
        total = total + parts[part].astype(F32)
    total = total.astype(BF)
    for place in range(held):
        buffer[place] = total
    copies = [
        pltpu.make_async_copy(buffer, out.at[first : first + held], sems.at[first // held])
        for first in range(0, count, held)
    ]
    for copy in copies:
        copy.start()
    for copy in copies:
        copy.wait()


def backward_kernel(dz, low, high, kernel, grads, wide):
    slabs, frames, rows, width, chans = dz.shape
    widen(wide, low[...], 0, True)
    widen(wide, dz[...], 1, True)
    widen(wide, high[...], rows + 1, True)
    per = rows * width
    planes = []
    for tap_t in range(3):
        total = jnp.zeros((slabs * frames * per, chans), F32)
        for tap_h in range(3):
            rows_in = wide[:, :, 2 - tap_h : 2 - tap_h + rows].reshape(slabs * frames * per, 3 * chans)
            at = 3 * (3 * tap_t + tap_h)
            weights = jnp.concatenate([kernel[at], kernel[at + 1], kernel[at + 2]], axis=1)
            total = total + lax.dot_general(rows_in, weights, (((1,), (1,)), ((), ())), preferred_element_type=F32)
        planes.append(total)
    for slab in range(slabs):
        for frame in range(frames + 2):
            total = None
            for tap_t in range(3):
                source = frame - tap_t
                if 0 <= source < frames:
                    at = (slab * frames + source) * per
                    term = planes[tap_t][at : at + per]
                    total = term if total is None else total + term
            grads[slab, frame] = total.astype(BF).reshape(rows, width, chans)


def vmem(count):
    return [pl.BlockSpec(memory_space=pltpu.VMEM)] * count


def smem(count):
    return [pl.BlockSpec(memory_space=pltpu.SMEM)] * count


def anywhere(count):
    return [pl.BlockSpec(memory_space=pl.ANY)] * count


def forward_call(lengths, low, high, clips, kernel):
    slabs, frames, rows, width, chans = clips.shape
    one = (frames - 2, rows, width, chans)
    return pl.pallas_call(
        forward_kernel,
        out_shape=(
            jax.ShapeDtypeStruct(one, BF),
            jax.ShapeDtypeStruct(one, BF),
            jax.ShapeDtypeStruct((slabs * (frames - 2) * rows * width, chans), F32),
        ),
        in_specs=smem(1) + anywhere(4),
        out_specs=tuple(vmem(3)),
        scratch_shapes=[
            pltpu.VMEM((slabs, frames, rows + 2, width, chans), BF),
            pltpu.VMEM(kernel.shape, BF),
            pltpu.VMEM((slabs, frames, rows + 2, width, 3 * chans), BF),
            pltpu.SemaphoreType.DMA((6,)),
        ],
        compiler_params=pltpu.CompilerParams(vmem_limit_bytes=32 * 2**20),
        name="forward",
    )(lengths, low, high, clips, kernel)


def weight_call(core, low, high, slope, cot_guest, clips, cot_stay):
    slabs, frames, rows, width, chans = clips.shape
    one = cot_stay.shape
    edge = (slabs, frames - 2, 1, width, chans)
    places = slabs * (frames - 2) * rows * width
    return pl.pallas_call(
        weight_kernel,
        out_shape=(
            jax.ShapeDtypeStruct((slabs,) + one, BF),
            jax.ShapeDtypeStruct(edge, BF),
            jax.ShapeDtypeStruct(edge, BF),
            jax.ShapeDtypeStruct((HALF_TAPS, chans, chans), BF),
            jax.ShapeDtypeStruct((slabs, frames, rows + 2, width, 3 * chans), BF),
            jax.ShapeDtypeStruct((chans, places), BF),
        ),
        in_specs=smem(1) + anywhere(4) + vmem(2),
        out_specs=tuple(vmem(6)),
        scratch_shapes=[
            pltpu.VMEM((2,) + low.shape, BF),
            pltpu.VMEM(slope.shape, F32),
            pltpu.VMEM(one, BF),
            pltpu.VMEM((16, chans, chans), F32),
            pltpu.SemaphoreType.DMA((4,)),
        ],
        compiler_params=pltpu.CompilerParams(vmem_limit_bytes=32 * 2**20),
        name="weights",
    )(core, low, high, slope, cot_guest, clips, cot_stay)


def mine_call(core, wide, turned):
    chans = turned.shape[0]
    return pl.pallas_call(
        mine_kernel,
        out_shape=jax.ShapeDtypeStruct((HALF_TAPS, chans, chans), F32),
        in_specs=smem(1) + vmem(2),
        out_specs=vmem(1)[0],
        scratch_shapes=[pltpu.VMEM((16, chans, chans), F32)],
        compiler_params=pltpu.CompilerParams(vmem_limit_bytes=32 * 2**20),
        name="mine",
    )(core, wide, turned)


def joined_call(mine, got):
    return pl.pallas_call(
        joined_kernel,
        out_shape=jax.ShapeDtypeStruct(mine.shape, BF),
        in_specs=vmem(2),
        out_specs=anywhere(1)[0],
        scratch_shapes=[pltpu.VMEM(mine.shape, BF), pltpu.SemaphoreType.DMA((2,))],
        compiler_params=pltpu.CompilerParams(vmem_limit_bytes=32 * 2**20),
        name="joined",
    )(mine, got)


def spread_call(parts, count):
    held = min(8, count)
    return pl.pallas_call(
        spread_kernel,
        out_shape=jax.ShapeDtypeStruct((count,) + parts.shape[1:], BF),
        in_specs=vmem(1),
        out_specs=anywhere(1)[0],
        scratch_shapes=[
            pltpu.VMEM((held,) + parts.shape[1:], BF),
            pltpu.SemaphoreType.DMA((count // held,)),
        ],
        compiler_params=pltpu.CompilerParams(vmem_limit_bytes=32 * 2**20),
        name="spread",
    )(parts)


def backward_call(dz, low, high, kernel):
    slabs, frames, rows, width, chans = dz.shape
    return pl.pallas_call(
        backward_kernel,
        out_shape=jax.ShapeDtypeStruct((slabs, frames + 2, rows, width, chans), BF),
        in_specs=vmem(4),
        out_specs=vmem(1)[0],
        scratch_shapes=[pltpu.VMEM((slabs, frames, rows + 2, width, 3 * chans), BF)],
        compiler_params=pltpu.CompilerParams(vmem_limit_bytes=32 * 2**20),
        name="backward",
    )(dz, low, high, kernel)


def write_taps(scale, first, rows, out, buffer, sems):
    pieces = ((0, 7), (7, HALF_TAPS - 1), (HALF_TAPS - 1, HALF_TAPS))
    copies = []
    for number, (low, high) in enumerate(pieces):
        buffer[low:high] = rows[low:high].astype(F32) * scale
        place = pl.ds(jnp.minimum(first[0] * HALF_TAPS + low, TAPS - (high - low)), high - low)
        copies.append(pltpu.make_async_copy(buffer.at[low:high], out.at[place], sems.at[number]))
        if number < 2:
            copies[-1].start()
        else:
            pl.when(first[0] == 0)(copies[-1].start)

    def wait():
        copies[0].wait()
        copies[1].wait()
        pl.when(first[0] == 0)(copies[2].wait)

    return wait


def half_kernel(scale, first, rows, passed, out, passed_out, buffer, held, sems):
    load = pltpu.make_async_copy(passed, held, sems.at[3])
    store = pltpu.make_async_copy(held, passed_out.at[0], sems.at[4])
    load.start()
    wait = write_taps(scale, first, rows, out, buffer, sems)
    load.wait()
    store.start()
    wait()
    store.wait()


def half_call(first, rows, scale, passed):
    return pl.pallas_call(
        functools.partial(half_kernel, scale),
        out_shape=(
            jax.ShapeDtypeStruct((TAPS,) + rows.shape[1:], F32),
            jax.ShapeDtypeStruct((1,) + passed.shape, passed.dtype),
        ),
        in_specs=smem(1) + vmem(1) + anywhere(1),
        out_specs=tuple(anywhere(2)),
        scratch_shapes=[
            pltpu.VMEM(rows.shape, F32),
            pltpu.VMEM(passed.shape, passed.dtype),
            pltpu.SemaphoreType.DMA((5,)),
        ],
        compiler_params=pltpu.CompilerParams(vmem_limit_bytes=32 * 2**20),
        name="own",
    )(first, rows, passed)


def rest_kernel(scale, first, rows, _, out, buffer, sems):
    write_taps(scale, first, rows, out, buffer, sems)()


def rest_call(first, rows, scale, earlier):
    return pl.pallas_call(
        functools.partial(rest_kernel, scale),
        out_shape=jax.ShapeDtypeStruct(earlier.shape, F32),
        in_specs=smem(1) + vmem(1) + anywhere(1),
        out_specs=anywhere(1)[0],
        scratch_shapes=[pltpu.VMEM(rows.shape, F32), pltpu.SemaphoreType.DMA((3,))],
        input_output_aliases={2: 0},
        compiler_params=pltpu.CompilerParams(vmem_limit_bytes=32 * 2**20),
        name="rest",
    )(first, rows, earlier)


def ring_hops(count):
    table = 0
    for mask in range(count):
        hops = [min((i ^ mask) - i & count - 1, i - (i ^ mask) & count - 1) for i in range(count)]
        table |= (sum(hops) // count) << (4 * mask)
    return table


def hops_of(mask, table):
    return jnp.bitwise_and(lax.shift_right_logical(jnp.int32(table), 4 * mask), 15)


def masks_of(axes, count):
    return [(axes, count, mask) for mask in range(count)]


def by_xor(value, masks, place, beside=None, extra=()):
    def branch(axes, count, mask):
        pairs = [(source, source ^ mask) for source in range(count)]

        def moved(item, *others):
            there = lax.ppermute(item, axes, pairs)
            return there if beside is None else (there, beside(*others))

        return moved

    return lax.switch(place, [branch(*entry) for entry in masks], value, *extra)


def swap_cores(value):
    return lax.ppermute(value, "c", [(0, 1), (1, 0)])


def shards(ny, nz, nx, scale, clips, lengths, partner, kernel, cot_stay, cot_guest):
    rows = clips.shape[2]
    chans = clips.shape[4]
    near = jnp.bitwise_and(partner[0], 2 * nz - 1)
    far = lax.shift_right_logical(partner[0], jnp.int32((2 * nz).bit_length() - 1))
    near_masks, far_masks = masks_of(("z", "c"), 2 * nz), masks_of("y", ny)
    far_first = hops_of(far, ring_hops(ny)) > hops_of(lax.shift_right_logical(near, jnp.int32(1)), ring_hops(nz))
    one_way, other_way = near, 2 * nz + far
    first_way = jnp.where(far_first, other_way, one_way)
    second_way = jnp.where(far_first, one_way, other_way)
    up = [(i, i + 1) for i in range(nx - 1)]
    down = [(i + 1, i) for i in range(nx - 1)]

    def edges(first, last):
        return lax.ppermute(last, "x", up), lax.ppermute(first, "x", down)

    core = lax.axis_index("c").astype(jnp.int32).reshape(1)
    first, last = lax.optimization_barrier((clips[:, :, :1], clips[:, :, rows - 1 :]))
    cot_here, (low, high) = by_xor(cot_guest[0], near_masks + far_masks, first_way, edges, (first, last))
    weights = kernel.reshape(9, 3 * chans, chans)
    cot_here, (y_stay, y_guest, slope) = by_xor(
        cot_here, near_masks + far_masks, second_way, forward_call, (lengths, low, high, clips, weights)
    )
    dz, dz_first, dz_last, other, wide, turned = weight_call(core, low, high, slope, cot_here, clips, cot_stay[0])
    half = joined_call(mine_call(core, wide, turned), swap_cores(other))
    parts = lax.all_to_all(half.reshape(ny * nx, -1, chans), ("y", "x"), 0, 0)
    guest = by_xor(y_guest, far_masks, far)
    parts, guest = lax.optimization_barrier((parts, guest))
    parts = lax.all_to_all(spread_call(parts, nz), "z", 0, 0)
    parts, dz_first, dz_last = lax.optimization_barrier((parts, dz_first, dz_last))
    whole = lax.all_to_all(spread_call(parts, ny * nx), ("y", "x"), 0, 0).reshape(half.shape)
    guest, (dz_low, dz_high) = by_xor(guest, near_masks, near, edges, (dz_first, dz_last))
    slab_grad = backward_call(dz, dz_low, dz_high, kernel.reshape(TAPS, chans, chans))
    whole, guest, slab_grad = lax.optimization_barrier((whole, guest, slab_grad))
    theirs = swap_cores(whole)
    weight_grad, guest = half_call(core, whole, scale, guest)
    weight_grad = rest_call(1 - core, theirs, scale, weight_grad).reshape(kernel.shape)
    return y_stay[None], guest, slab_grad, weight_grad


def solution(mesh):
    nx = mesh.shape["space"]
    ny = nz = math.isqrt(mesh.shape["dp"] // 2)
    fine = Mesh(mesh.devices.reshape(ny, nz, 2, nx), ("y", "z", "c", "x"))
    block = P(("y", "z", "c"), None, "x", None, None)

    def whole(clips, lengths, partner, kernel, cot_stay, cot_guest):
        slabs, _, height, width, _ = clips.shape
        scale = 1.0 / math.sqrt(slabs * cot_stay.shape[1] * height * width)
        return jax.shard_map(
            functools.partial(shards, ny, nz, nx, scale),
            mesh=fine,
            in_specs=(block, P(("y", "z", "c")), P(), P(), block, block),
            out_specs=(block, block, block, P()),
            check_vma=False,
        )(clips, lengths, partner, kernel, cot_stay, cot_guest)

    return whole
```
